512 devices in a mesh: clip: 64 (over z_hi, y, x), space: 8 (over z_lo, core).
Axes of the slice: x: 4, y: 8, z: 8 (z_hi: 2, z_lo: 4; z = z_hi * 4 + z_lo), core: 2. Of those that a mesh axis runs over, the one named last changes fastest.
Arguments:
- latent: bfloat16 [512, 256, 640], P('clip', 'space'), may hold values from -6 to 6
- spatial_qkv: bfloat16 [640, 960], replicated, may hold values from -2.1875 to 2.1875
- spatial_out: bfloat16 [320, 640], replicated, may hold values from -0.3125 to 0.3125
- temporal_qkv: bfloat16 [640, 960], replicated, may hold values from -2.1875 to 2.1875
- temporal_out: bfloat16 [320, 640], replicated, may hold values from -0.3125 to 0.3125
Outputs:
- latent_out: bfloat16 [512, 256, 640], P('clip', 'space')
The draws below stay inside these ranges and needn't reach their ends.
All inputs are finite; a program needn't handle non-finite values.
Results may differ from the reference program's by a relative error of at most 0.012.
Values may be sent and summed in bfloat16 or wider, within the bound.
A program may use at most 128 MiB of HBM per device.

```python
import jax
import jax.numpy as jnp
from jax import lax

C = 640
HEADS = 5
INNER = 320
FRAMES = 8
CTX = 2
POS = 256
VIDEO = 512
N_CLIP = 64


def drawn_qkv(key):
    return jax.random.truncated_normal(key, -4.0, 4.0, (C, 3 * INNER), jnp.float32) * C ** (-0.5)


def draw_spatial_qkv(key, part):
    key = jax.random.fold_in(key, 1)
    return drawn_qkv(key).astype(jnp.bfloat16)


def draw_temporal_qkv(key, part):
    key = jax.random.fold_in(key, 2)
    return drawn_qkv(key).astype(jnp.bfloat16)


def block_scale(stream_key, dims, shards, smallest, largest):
    loudness = 1.0
    for position, shards_of in shards:
        steps = jax.random.uniform(jax.random.fold_in(jax.random.fold_in(stream_key, 6), position), (shards_of,), jnp.float32, smallest / len(shards), largest / len(shards))
        loudness = loudness * jnp.repeat(jnp.exp(steps), dims[position] // shards_of).reshape((-1,) + (1,) * (len(dims) - 1 - position))
    return loudness


def normal_values(stream_key, shape, deviation, most, pieces=(), kind=jnp.bfloat16):
    loudness = block_scale(stream_key, shape, pieces, -0.22, 0.18) if pieces else 1.0
    array = jax.random.normal(stream_key, shape, jnp.float32) * deviation * loudness
    return jnp.minimum(jnp.maximum(array, -most), most).astype(kind)


def setup_inputs(seed: int = 0) -> dict:
    key_list = jax.random.split(jax.random.key(seed), 6)
    latent = normal_values(key_list[0], (VIDEO, POS, C), 1.0, 6.0, ((0, 64), (1, 8)))
    spatial_qkv = draw_spatial_qkv(jax.random.fold_in(key_list[5], 71), 0)
    spatial_out = normal_values(key_list[2], (INNER, C), INNER ** -0.5, 0.3125)
    temporal_qkv = draw_temporal_qkv(jax.random.fold_in(key_list[5], 71), 0)
    temporal_out = normal_values(key_list[4], (INNER, C), INNER ** -0.5, 0.3125)
    return dict(latent=latent, spatial_qkv=spatial_qkv, spatial_out=spatial_out, temporal_qkv=temporal_qkv, temporal_out=temporal_out)


def normalize(values):
    widened = values.astype(jnp.float32)
    center = widened - lax.optimization_barrier(jnp.mean(widened, axis=-1, keepdims=True))
    spread = lax.optimization_barrier(jnp.mean(center * center, axis=-1, keepdims=True))
    return (center * lax.rsqrt(spread + 1e-05)).astype(jnp.bfloat16)

def project(values, weight):
    flat_rows = values.reshape(-1, values.shape[-1])
    output = jnp.dot(flat_rows, weight, preferred_element_type=jnp.float32)
    return output.reshape(values.shape[:-1] + (weight.shape[1],))

def attend_space(queries, key_value):
    frame_count, row_count, inner_width = queries.shape
    key_count = key_value.shape[1]
    head_dim = inner_width // HEADS
    query_heads = queries.reshape(frame_count, row_count, HEADS, head_dim).astype(jnp.float32)
    key_heads = key_value[..., :inner_width].reshape(frame_count, key_count, HEADS, head_dim).astype(jnp.float32)
    value_heads = key_value[..., inner_width:].reshape(frame_count, key_count, HEADS, head_dim).astype(jnp.float32)
    scores = jnp.einsum('fqhd,fkhd->fhqk', query_heads, key_heads) * head_dim ** (-0.5)
    weights = jax.nn.softmax(scores, axis=-1).astype(jnp.bfloat16)
    mixed = jnp.einsum('fhqk,fkhd->fqhd', weights.astype(jnp.float32), value_heads)
    return mixed.astype(jnp.bfloat16).reshape(frame_count, row_count, inner_width)

def attend_time(queries, key_value, allowed):
    frame_count, row_count, inner_width = queries.shape
    key_count = key_value.shape[0]
    head_dim = inner_width // HEADS
    query_heads = queries.reshape(frame_count, row_count, HEADS, head_dim).astype(jnp.float32)
    key_heads = key_value[..., :inner_width].reshape(key_count, row_count, HEADS, head_dim).astype(jnp.float32)
    value_heads = key_value[..., inner_width:].reshape(key_count, row_count, HEADS, head_dim).astype(jnp.float32)
    scores = jnp.einsum('fphd,kphd->phfk', query_heads, key_heads) * head_dim ** (-0.5)
    scores = jnp.where(allowed, scores, -1e+30)
    weights = jax.nn.softmax(scores, axis=-1).astype(jnp.bfloat16)
    mixed = jnp.einsum('phfk,kphd->fphd', weights.astype(jnp.float32), value_heads)
    return mixed.astype(jnp.bfloat16).reshape(frame_count, row_count, inner_width)

def reference(latent, spatial_qkv, spatial_out, temporal_qkv, temporal_out):
    video = latent.reshape(N_CLIP, FRAMES, POS, C)

    def space_step(frame_block):
        packed = project(normalize(frame_block), spatial_qkv).astype(jnp.bfloat16)
        mixed = attend_space(packed[..., :INNER], packed[..., INNER:])
        return (frame_block.astype(jnp.float32) + project(mixed, spatial_out)).astype(jnp.bfloat16)
    spatial = lax.map(space_step, video)

    def qkv_step(frame_block):
        return project(normalize(frame_block), temporal_qkv).astype(jnp.bfloat16)
    packed = lax.map(qkv_step, spatial)
    key_value = packed[..., INNER:]
    anchors = key_value[:, 0]
    blank = jnp.zeros((1,) + key_value.shape[1:], jnp.bfloat16)
    padded = jnp.concatenate([blank, key_value, blank], axis=0)
    key_slots = jnp.arange(FRAMES + 2 * CTX + N_CLIP, dtype=jnp.int32)

    def time_step(clip_index):
        window = lax.dynamic_slice_in_dim(padded, clip_index, 3, 0)
        gathered = jnp.concatenate([window[0, FRAMES - CTX:], window[1], window[2, :CTX], anchors], axis=0)
        allowed = ((key_slots >= CTX) | (clip_index > 0)) & ((key_slots < FRAMES + CTX) | (key_slots >= FRAMES + 2 * CTX) | (clip_index < N_CLIP - 1))
        own_packed = lax.dynamic_index_in_dim(packed, clip_index, 0, keepdims=False)
        own_spatial = lax.dynamic_index_in_dim(spatial, clip_index, 0, keepdims=False)
        mixed = attend_time(own_packed[..., :INNER], gathered, allowed)
        return (own_spatial.astype(jnp.float32) + project(mixed, temporal_out)).astype(jnp.bfloat16)
    result = lax.map(time_step, jnp.arange(N_CLIP, dtype=jnp.int32))
    return result.reshape(VIDEO, POS, C)
```

```python
import jax
import jax.numpy as jnp
from jax import lax
from jax.experimental import pallas as pl
from jax.experimental.pallas import tpu as pltpu
from jax.sharding import PartitionSpec as P

MESH = pl.DeviceIdType.MESH
HEADS = 5
NZ, NY, NX = 2, 8, 4
N_CLIP = NZ * NY * NX
NS = 8
FRAMES = 8
ROWS = 32
HALF = 16
C = 640
INNER = 320
WIDE = 384
COPIES = 112
NEG = -1e30
BF = jnp.bfloat16
F32 = jnp.float32


def wrap(value, count):
    return lax.rem(value + 2 * count, count)


def normalize(values):
    wide = values.astype(F32)
    center = wide - jnp.mean(wide, axis=-1, keepdims=True)
    spread = jnp.mean(center * center, axis=-1, keepdims=True)
    return (center * lax.rsqrt(spread + 1e-05)).astype(BF)


def dot(a, b):
    return jnp.dot(a, b, preferred_element_type=F32)


def dot_t(a, b):
    return lax.dot_general(a, b, (((1,), (1,)), ((), ())), preferred_element_type=F32)


def low_lanes(rows):
    return lax.broadcasted_iota(jnp.int32, (rows, 128), 1) < 64


def head_queries(qkv):
    low = low_lanes(qkv.shape[0])
    tiles = []
    for h in range(HEADS):
        tile = qkv[:, 128 * (h // 2):128 * (h // 2) + 128].astype(F32) * 0.125
        keep = low if h % 2 == 0 else jnp.logical_not(low)
        tiles.append(jnp.where(keep, tile, 0.0).astype(BF))
    return tiles


def side_by_side(heads):
    low = low_lanes(heads[0].shape[0])
    return jnp.concatenate(
        [
            jnp.where(low, 0.0, heads[0]),
            jnp.where(low, heads[1], heads[2]),
            jnp.where(low, heads[3], heads[4]),
        ],
        axis=1,
    )


def attend_space(queries, kv):
    heads = []
    for h in range(HEADS):
        kt, vt = 128 * (h // 2), 128 * (2 + (h + 1) // 2)
        scores = dot_t(queries[h], kv[:, kt:kt + 128])
        p = jnp.exp(scores - jnp.max(scores, axis=-1, keepdims=True))
        total = jnp.sum(p, axis=-1, keepdims=True)
        heads.append(dot(p.astype(BF), kv[:, vt:vt + 128]) / total)
    return side_by_side(heads).astype(BF)


def kernel(lat_h, wsq_h, wso_h, wtq_h, wto_h, out_ref,
           lat, wsq, wso, wtq, wto, f0, fr, kvs, q0, sa_out, sa_in, anc, tkv, prev, nxt,
           spat, qm, acc, top, tot, tatt, lsem, ssem, rsem):
    clip = lax.axis_index("clip")
    s = lax.axis_index("space")
    zh, y, x = clip // (NY * NX), (clip // NX) % NY, clip % NX
    zl, core = s // 2, s % 2

    def at_clip(z_, y_, x_):
        return {"clip": (z_ * NY + y_) * NX + x_, "space": s}

    def at_space(s_):
        return {"clip": clip, "space": s_}

    partner = at_clip(1 - zh, y, x)
    x_peer = {d: at_clip(zh, y, wrap(x + d, NX)) for d in (1, 2, 3)}
    y_peer = {d: at_clip(zh, wrap(y + d, NY), x) for d in (1, -1)}
    following = {"clip": wrap(clip + 1, N_CLIP), "space": s}
    preceding = {"clip": wrap(clip - 1, N_CLIP), "space": s}

    local = []
    wso[0:64, :] = jnp.zeros((64, C), BF)
    wto[0:64, :] = jnp.zeros((64, C), BF)
    for i, (src, dst) in enumerate([
        (lat_h, lat), (wsq_h, wsq), (wso_h, wso.at[pl.ds(64, INNER)]), (wtq_h, wtq), (wto_h, wto.at[pl.ds(64, INNER)]),
    ]):
        copy = pltpu.make_async_copy(src, dst, lsem.at[i])
        copy.start()
        local.append(copy)
    barrier = pltpu.get_barrier_semaphore()
    partners = [at_space(wrap(s + d, NS)) for d in range(1, NS)]
    partners += [partner, x_peer[1], x_peer[2], x_peer[3], y_peer[1], y_peer[-1], following, preceding]
    for device in partners:
        pl.semaphore_signal(barrier, inc=1, device_id=device, device_id_type=MESH)
    local[0].wait()
    f0[s] = lat[0]
    fr[s] = lat[s]
    pl.semaphore_wait(barrier, len(partners))

    count = [0]
    sent = []

    def number():
        count[0] += 1
        return count[0] - 1

    def make(i, src, dst, device):
        return pltpu.make_async_remote_copy(
            src_ref=src, dst_ref=dst, send_sem=ssem.at[i], recv_sem=rsem.at[i], device_id=device, device_id_type=MESH
        )

    def send(i, ref, device, dst=None):
        copy = make(i, ref, ref if dst is None else dst, device)
        copy.start()
        sent.append(copy)

    def recv(i, ref, device):
        make(i, ref, ref, device).wait_recv()

    sibling = at_space(zl * 2 + 1 - core)
    same_core = {d: at_space(wrap(zl + d, 4) * 2 + core) for d in (1, 2, 3)}
    mine = f0.at[s]
    n_direct = {d: number() for d in (1, 2, 3)}
    n_relay = {d: number() for d in (1, 2, 3)}
    n_sib = number()
    for d in (2, 1, 3):
        send(n_direct[d], mine, same_core[d])
    send(n_sib, mine, sibling)
    for d in (1, 3, 2):
        slot = f0.at[wrap(zl - d, 4) * 2 + core]
        recv(n_direct[d], slot, same_core[d])
        send(n_relay[d], slot, sibling)

    n_frame = {d: number() for d in range(1, NS)}
    n_back = {d: number() for d in range(1, NS)}

    conditional = []

    def send_if(cond, i, src, device, dst):
        copy = make(i, src, dst, device)

        @pl.when(cond)
        def _():
            copy.start()

        conditional.append((cond, copy))

    for d in range(1, NS):
        owner = wrap(s + d, NS)
        send_if(owner != 0, n_frame[d], lat.at[owner], at_space(owner), fr.at[s])

    recv(n_sib, f0.at[zl * 2 + 1 - core], sibling)
    for d in (1, 3, 2):
        recv(n_relay[d], f0.at[wrap(zl - d, 4) * 2 + 1 - core], sibling)

    def temporal_rows(latent, attn, first, frames):
        rows = frames * ROWS
        spatial = (latent.astype(F32) + dot(attn, wso[...])).astype(BF)
        spat[pl.ds(first, frames)] = spatial.reshape(frames, ROWS, C)
        qkv = dot(normalize(spatial), wtq[...]).astype(BF)
        kv = qkv[:, INNER:]
        tkv[pl.ds(first, frames)] = kv.reshape(frames, ROWS, 2 * INNER)
        for h, tile in enumerate(head_queries(qkv)):
            tile = tile.reshape(frames, ROWS, 128)
            for g in range(2):
                qm[g, h, pl.ds(first, frames)] = tile[:, HALF * g:HALF * g + HALF]
        return kv

    local[1].wait()
    qkv0 = dot(normalize(f0[...].reshape(NS * ROWS, C)), wsq[...]).astype(BF)
    q0[...] = qkv0[:, :WIDE].reshape(NS, ROWS, WIDE)
    mixed0 = attend_space(head_queries(q0[s]), qkv0[:, INNER:])
    for copy in local[2:]:
        copy.wait()
    kv0 = temporal_rows(lat[0], mixed0, 0, 1)
    anc[0, y, NX * zh + x] = kv0[:HALF]
    anc[1, NZ * x + zh, y] = kv0[HALF:]

    planes = (zh, 1 - zh)
    n_za, n_zb = number(), number()
    n_xa = {(p, d): number() for p in range(2) for d in (1, 2, 3)}
    n_ya = {(p, k, d): number() for p in range(2) for k in range(4) for d in (1, -1)}
    n_yb = {(p, k, d): number() for p in range(2) for k in range(4) for d in (1, -1)}
    n_xb = {(p, k, d): number() for p in range(2) for k in range(2) for d in (1, -1)}

    def send_xa(p):
        for d in (2, 1, 3):
            send(n_xa[p, d], anc.at[0, y, NX * planes[p] + x], x_peer[d])

    def recv_xa(p):
        for d in (1, 3, 2):
            recv(n_xa[p, d], anc.at[0, y, NX * planes[p] + wrap(x - d, NX)], x_peer[d])

    def row_a(p, yy, k, d):
        if k < 3:
            return anc.at[0, yy, pl.ds(NX * planes[p], NX)]
        return anc.at[0, yy, pl.ds(NX * planes[p] + (0 if d == 1 else 2), 2)]

    def send_ya(p, k):
        for d in (1, -1):
            send(n_ya[p, k, d], row_a(p, wrap(y - d * k, NY), k, d), y_peer[d])

    def recv_ya(p, k):
        for d in (1, -1):
            recv(n_ya[p, k, d], row_a(p, wrap(y - d * (k + 1), NY), k, d), y_peer[d])

    def ways_b(p, k):
        return (1, -1) if k < 3 else ((1,) if p == 0 else (-1,))

    def send_yb(p, k):
        for d in ways_b(p, k):
            send(n_yb[p, k, d], anc.at[1, NZ * x + planes[p], wrap(y - d * k, NY)], y_peer[d])

    def recv_yb(p, k):
        for d in ways_b(p, k):
            recv(n_yb[p, k, d], anc.at[1, NZ * x + planes[p], wrap(y - d * (k + 1), NY)], y_peer[d])

    def col_b(p, xx, k, d):
        if k == 0:
            return anc.at[1, NZ * xx + planes[p]]
        return anc.at[1, NZ * xx + planes[p], pl.ds(0 if d == 1 else 4, 4)]

    def send_xb(p, k):
        for d in (1, -1):
            send(n_xb[p, k, d], col_b(p, wrap(x - d * k, NX), k, d), x_peer[1 if d == 1 else 3])

    def recv_xb(p, k):
        for d in (1, -1):
            recv(n_xb[p, k, d], col_b(p, wrap(x - d * (k + 1), NX), k, d), x_peer[1 if d == 1 else 3])

    send(n_za, anc.at[0, y, NX * zh + x], partner)
    send(n_zb, anc.at[1, NZ * x + zh, y], partner)
    send_yb(0, 0)
    send_xa(0)

    recv_xa(0)
    send_ya(0, 0)
    recv_yb(0, 0)
    send_yb(0, 1)
    recv(n_za, anc.at[0, y, NX * (1 - zh) + x], partner)
    send_xa(1)
    recv(n_zb, anc.at[1, NZ * x + 1 - zh, y], partner)
    send_yb(1, 0)
    recv_yb(0, 1)
    send_yb(0, 2)
    recv_xa(1)
    send_ya(1, 0)
    recv_yb(1, 0)
    send_yb(1, 1)
    recv_yb(0, 2)
    send_yb(0, 3)
    recv_yb(1, 1)
    send_yb(1, 2)

    @pl.when(s != 0)
    def _():
        for d in range(1, NS):
            recv(n_frame[d], fr.at[wrap(s - d, NS)], at_space(wrap(s + d, NS)))
        qkv = dot(normalize(fr[...].reshape(NS * ROWS, C)), wsq[...]).astype(BF)
        kvs[...] = qkv[:, INNER:]
        mixed = attend_space(head_queries(qkv), kvs[...])
        sa_out[...] = mixed.reshape(NS, ROWS, WIDE)
        sa_in[s] = sa_out[s]

    for d in range(1, NS):
        there = wrap(s + d, NS)
        send_if(s != 0, n_back[d], sa_out.at[there], at_space(there), sa_in.at[s])

    recv_yb(0, 3)
    send_xb(0, 0)
    recv_ya(0, 0)
    send_ya(0, 1)
    recv_yb(1, 2)
    send_yb(1, 3)
    recv_ya(1, 0)
    send_ya(1, 1)

    for d in range(1, NS):
        owner = wrap(s - d, NS)

        @pl.when(owner != 0)
        def _():
            recv(n_back[d], sa_in.at[owner], at_space(owner))

    rest = FRAMES - 1
    temporal_rows(
        lat[1:].reshape(rest * ROWS, C), sa_in[1:].reshape(rest * ROWS, WIDE), 1, rest
    )
    n_next, n_prev = number(), number()
    send(n_next, tkv.at[pl.ds(FRAMES - 2, 2)], following, prev)
    send(n_prev, tkv.at[pl.ds(0, 2)], preceding, nxt)

    recv_yb(1, 3)
    send_xb(1, 0)
    recv_ya(0, 1)
    send_ya(0, 2)

    def same_position(keys):
        rows = lax.broadcasted_iota(jnp.int32, (HEADS * FRAMES * HALF, keys), 0) % HALF
        return rows == lax.broadcasted_iota(jnp.int32, (HEADS * FRAMES * HALF, keys), 1) % HALF

    block = FRAMES * HALF

    def attend(g, load, keys, allowed=None, start=False):
        queries = qm[g].reshape(HEADS * block, 128)
        tiles = [load(t) for t in range(5)]
        scores = jnp.concatenate(
            [
                dot_t(queries[:2 * block], tiles[0]),
                dot_t(queries[2 * block:4 * block], tiles[1]),
                dot_t(queries[4 * block:], tiles[2]),
            ],
            axis=0,
        )
        mask = same_position(keys)
        if allowed is not None:
            mask = jnp.logical_and(mask, allowed)
        scores = jnp.where(mask, scores, NEG)
        high = jnp.max(scores, axis=-1, keepdims=True)
        if not start:
            high = jnp.maximum(high, top[g])
        p = jnp.exp(scores - high)
        total = jnp.sum(p, axis=-1, keepdims=True)
        p = p.astype(BF)
        out = jnp.concatenate(
            [dot(p[:block], tiles[2]), dot(p[block:3 * block], tiles[3]), dot(p[3 * block:], tiles[4])], axis=0
        )
        if not start:
            shrink = jnp.exp(top[g] - high)
            total = total + tot[g] * shrink
            out = out + acc[g] * shrink
        top[g] = high
        tot[g] = total
        acc[g] = out

    def lanes(t):
        return pl.ds(128 * t, 128)

    def window(g):
        at = pl.ds(pl.multiple_of(HALF * g, HALF), HALF)

        def load(t):
            pieces = [r[:, at, lanes(t)] for r in (tkv, prev, nxt)]
            return jnp.concatenate([r.reshape(r.shape[0] * HALF, 128) for r in pieces], axis=0)
        return load

    def attend_window(g):
        keys = (FRAMES + 4) * HALF
        key = lax.broadcasted_iota(jnp.int32, (HEADS * block, keys), 1)
        first = jnp.where(clip > 0, block, block + 2 * HALF)
        last = jnp.where(clip < N_CLIP - 1, block + 4 * HALF, block + 2 * HALF)
        attend(g, window(g), keys, allowed=(key < block) | ((key >= first) & (key < last)))

    def attend_anchors(g, c, start=False):
        column = NZ * wrap(x + (0, 1, -1, 2)[c], NX)
        one = jnp.where(g == 0, wrap(y - c, NY), column)
        two = jnp.where(g == 0, wrap(y + c + 1, NY), column + 1)

        def load(t):
            return jnp.concatenate([anc[g, r, :, :, lanes(t)].reshape(block, 128) for r in (one, two)], axis=0)
        attend(g, load, 2 * block, start=start)

    def both(body, *args):
        def run(g, carry):
            body(g, *args)
            return carry
        lax.fori_loop(0, 2, run, 0)

    recv_ya(1, 1)
    send_ya(1, 2)
    recv_xb(0, 0)
    send_xb(0, 1)
    both(attend_anchors, 0, True)
    recv_ya(0, 2)
    send_ya(0, 3)
    recv_xb(1, 0)
    send_xb(1, 1)
    recv_ya(1, 2)
    send_ya(1, 3)
    both(attend_anchors, 1)
    recv(n_next, prev, preceding)
    recv(n_prev, nxt, following)
    both(attend_window)
    both(attend_anchors, 2)
    recv_ya(0, 3)
    recv_ya(1, 3)
    recv_xb(0, 1)
    recv_xb(1, 1)
    both(attend_anchors, 3)

    for g in range(2):
        mixed = acc[g] / tot[g]
        mixed = side_by_side([mixed[h * block:(h + 1) * block] for h in range(HEADS)]).astype(BF)
        tatt[:, g] = mixed.reshape(FRAMES, HALF, WIDE)
    update = dot(tatt[...].reshape(FRAMES * ROWS, WIDE), wto[...])
    out = (spat[...].reshape(FRAMES * ROWS, C).astype(F32) + update).astype(BF)
    out_ref[...] = out.reshape(FRAMES, ROWS, C)

    for copy in sent:
        copy.wait_send()
    for cond, copy in conditional:
        @pl.when(cond)
        def _():
            copy.wait_send()
    assert count[0] <= COPIES


def step(latent, spatial_qkv, spatial_out, temporal_qkv, temporal_out):
    vmem = pltpu.VMEM
    tokens = FRAMES * HALF
    return pl.pallas_call(
        kernel,
        out_shape=jax.ShapeDtypeStruct(latent.shape, BF),
        in_specs=[pl.BlockSpec(memory_space=pl.ANY)] * 5,
        out_specs=pl.BlockSpec(memory_space=pltpu.VMEM),
        scratch_shapes=[
            vmem((FRAMES, ROWS, C), BF),
            vmem((C, 3 * INNER), BF),
            vmem((WIDE, C), BF),
            vmem((C, 3 * INNER), BF),
            vmem((WIDE, C), BF),
            vmem((NS, ROWS, C), BF),
            vmem((NS, ROWS, C), BF),
            vmem((NS * ROWS, 2 * INNER), BF),
            vmem((NS, ROWS, WIDE), BF),
            vmem((NS, ROWS, WIDE), BF),
            vmem((FRAMES, ROWS, WIDE), BF),
            vmem((2, 8, 8, HALF, 2 * INNER), BF),
            vmem((FRAMES, ROWS, 2 * INNER), BF),
            vmem((2, ROWS, 2 * INNER), BF),
            vmem((2, ROWS, 2 * INNER), BF),
            vmem((FRAMES, ROWS, C), BF),
            vmem((2, HEADS, FRAMES, HALF, 128), BF),
            vmem((2, HEADS * tokens, 128), F32),
            vmem((2, HEADS * tokens, 1), F32),
            vmem((2, HEADS * tokens, 1), F32),
            vmem((FRAMES, 2, HALF, WIDE), BF),
            pltpu.SemaphoreType.DMA((5,)),
            pltpu.SemaphoreType.DMA((COPIES,)),
            pltpu.SemaphoreType.DMA((COPIES,)),
        ],
        compiler_params=pltpu.CompilerParams(
            collective_id=0, has_side_effects=True, vmem_limit_bytes=40 * 1024 * 1024
        ),
        name="denoise",
    )(latent, spatial_qkv, spatial_out, temporal_qkv, temporal_out)


def solution(mesh):
    in_specs = (P("clip", "space", None), P(), P(), P(), P())
    out_specs = P("clip", "space", None)
    return jax.shard_map(step, mesh=mesh, in_specs=in_specs, out_specs=out_specs, check_vma=False)
```

```python
import jax
import jax.numpy as jnp
from jax import lax
from jax.experimental import pallas as pl
from jax.experimental.pallas import tpu as pltpu
from jax.sharding import PartitionSpec as P

MESH = pl.DeviceIdType.MESH
HEADS = 5
NZ, NY, NX = 2, 8, 4
N_CLIP = NZ * NY * NX
NS = 8
FRAMES = 8
ROWS = 32
HALF = 16
C = 640
INNER = 320
WIDE = 384
COPIES = 112
NEG = -1e30
BF = jnp.bfloat16
F32 = jnp.float32


def wrap(value, count):
    return lax.rem(value + 2 * count, count)


def normalize(values):
    wide = values.astype(F32)
    center = wide - jnp.mean(wide, axis=-1, keepdims=True)
    spread = jnp.mean(center * center, axis=-1, keepdims=True)
    return (center * lax.rsqrt(spread + 1e-05)).astype(BF)


def dot(a, b):
    return jnp.dot(a, b, preferred_element_type=F32)


def dot_t(a, b):
    return lax.dot_general(a, b, (((1,), (1,)), ((), ())), preferred_element_type=F32)


def low_lanes(rows):
    return lax.broadcasted_iota(jnp.int32, (rows, 128), 1) < 64


def head_queries(queries):
    low = low_lanes(queries.shape[0])
    tiles = []
    for h in range(HEADS):
        tile = queries[:, 128 * (h // 2):128 * (h // 2) + 128].astype(BF).astype(F32) * 0.125
        keep = low if h % 2 == 0 else jnp.logical_not(low)
        tiles.append(jnp.where(keep, tile, 0.0).astype(BF))
    return tiles


def side_by_side(heads):
    low = low_lanes(heads[0].shape[0])
    return jnp.concatenate(
        [
            jnp.where(low, 0.0, heads[0]),
            jnp.where(low, heads[1], heads[2]),
            jnp.where(low, heads[3], heads[4]),
        ],
        axis=1,
    )


def attend_space(queries, kv):
    heads = []
    for h in range(HEADS):
        kt, vt = 128 * (h // 2), 128 * (2 + (h + 1) // 2)
        scores = dot_t(queries[h], kv[:, kt:kt + 128])
        p = jnp.exp(scores - jnp.max(scores, axis=-1, keepdims=True))
        total = jnp.sum(p, axis=-1, keepdims=True)
        heads.append(dot(p.astype(BF), kv[:, vt:vt + 128]) / total)
    return side_by_side(heads).astype(BF)


def kernel(lat_h, wsq_h, wso_h, wtq_h, wto_h, out_ref,
           lat, wsq, wso, wtq, wto, f0, fr, kvs, sa_out, sa_in, anc, tkv, prev, nxt,
           spat, qm, acc, top, tot, tatt, lsem, ssem, rsem):
    clip = lax.axis_index("clip")
    s = lax.axis_index("space")
    zh, y, x = clip // (NY * NX), (clip // NX) % NY, clip % NX
    zl, core = s // 2, s % 2

    def at_clip(z_, y_, x_):
        return {"clip": (z_ * NY + y_) * NX + x_, "space": s}

    def at_space(s_):
        return {"clip": clip, "space": s_}

    partner = at_clip(1 - zh, y, x)
    x_peer = {d: at_clip(zh, y, wrap(x + d, NX)) for d in (1, 2, 3)}
    y_peer = {d: at_clip(zh, wrap(y + d, NY), x) for d in range(1, NY)}
    following = {"clip": wrap(clip + 1, N_CLIP), "space": s}
    preceding = {"clip": wrap(clip - 1, N_CLIP), "space": s}

    barrier = pltpu.get_barrier_semaphore()
    partners = [at_space(wrap(s + d, NS)) for d in range(1, NS)]
    partners += [partner] + [x_peer[d] for d in (1, 2, 3)] + [y_peer[d] for d in range(1, NY)] + [following, preceding]
    for device in partners:
        pl.semaphore_signal(barrier, inc=1, device_id=device, device_id_type=MESH)
    local = []

    def fetch(*pairs):
        for src, dst in pairs:
            copy = pltpu.make_async_copy(src, dst, lsem.at[len(local)])
            copy.start()
            local.append(copy)

    fetch((lat_h, lat))
    wso[0:64, :] = jnp.zeros((64, C), BF)
    wto[0:64, :] = jnp.zeros((64, C), BF)
    pl.semaphore_wait(barrier, len(partners))

    count = [0]
    sent = []

    def number():
        count[0] += 1
        return count[0] - 1

    def make(i, src, dst, device):
        return pltpu.make_async_remote_copy(
            src_ref=src, dst_ref=dst, send_sem=ssem.at[i], recv_sem=rsem.at[i], device_id=device, device_id_type=MESH
        )

    def send(i, ref, device, dst=None):
        copy = make(i, ref, ref if dst is None else dst, device)
        copy.start()
        sent.append(copy)

    def recv(i, ref, device):
        make(i, ref, ref, device).wait_recv()

    sibling = at_space(zl * 2 + 1 - core)
    same_core = {d: at_space(wrap(zl + d, 4) * 2 + core) for d in (1, 2, 3)}
    mine = lat_h.at[0]
    n_direct = {d: number() for d in (1, 2, 3)}
    n_relay = {d: number() for d in (1, 2, 3)}
    n_sib = number()
    for d in (2, 1, 3):
        send(n_direct[d], mine, same_core[d], f0.at[s])
    send(n_sib, mine, sibling, f0.at[s])
    fetch((wsq_h, wsq), (wso_h, wso.at[pl.ds(64, INNER)]), (wtq_h, wtq), (wto_h, wto.at[pl.ds(64, INNER)]))
    local[0].wait()
    f0[s] = lat[0]
    fr[s] = lat[s]
    for d in (1, 3, 2):
        slot = f0.at[wrap(zl - d, 4) * 2 + core]
        recv(n_direct[d], slot, same_core[d])
        send(n_relay[d], slot, sibling)

    n_frame = {d: number() for d in range(1, NS)}
    n_back = {d: number() for d in range(1, NS)}

    conditional = []

    def send_if(cond, i, src, device, dst):
        copy = make(i, src, dst, device)

        @pl.when(cond)
        def _():
            copy.start()

        conditional.append((cond, copy))

    for d in range(1, NS):
        owner = wrap(s + d, NS)
        send_if(owner != 0, n_frame[d], lat_h.at[owner], at_space(owner), fr.at[s])

    recv(n_sib, f0.at[zl * 2 + 1 - core], sibling)
    for d in (1, 3, 2):
        recv(n_relay[d], f0.at[wrap(zl - d, 4) * 2 + 1 - core], sibling)

    def temporal_rows(latent, attn, first, frames):
        rows = frames * ROWS
        spatial = (latent.astype(F32) + dot(attn, wso[...])).astype(BF)
        spat[pl.ds(first, frames)] = spatial.reshape(frames, ROWS, C)
        normed = normalize(spatial)
        kv = dot_t(normed, wtq[INNER:]).astype(BF)
        tkv[pl.ds(first, frames)] = kv.reshape(frames, ROWS, 2 * INNER)
        return kv, normed

    def temporal_queries(normed, first, frames):
        for h, tile in enumerate(head_queries(dot_t(normed, wtq[:WIDE]))):
            tile = tile.reshape(frames, ROWS, 128)
            for g in range(2):
                qm[g, h, pl.ds(first, frames)] = tile[:, HALF * g:HALF * g + HALF]

    local[1].wait()
    queries0 = head_queries(dot_t(normalize(lat[0]), wsq[:WIDE]))
    kvs[...] = dot_t(normalize(f0[...].reshape(NS * ROWS, C)), wsq[INNER:]).astype(BF)
    mixed0 = attend_space(queries0, kvs)
    for copy in local[2:]:
        copy.wait()
    kv0, normed0 = temporal_rows(lat[0], mixed0, 0, 1)
    anc[0, y // 2, (y % 2) * NX + x] = kv0[:HALF]
    anc[1, NZ * x, y] = kv0[HALF:]

    def cell(part, xx, yy):
        if part == 0:
            return anc.at[0, yy // 2, (yy % 2) * NX + xx]
        if part == 1:
            return anc.at[0, NX + xx, yy]
        return anc.at[1, NZ * xx + part - 2, yy]

    def column(part, xx, *half):
        ref = anc.at[0, NX + xx] if part == 1 else anc.at[1, NZ * xx + part - 2]
        return ref.at[pl.ds(*half)] if half else ref

    def line(yy, k, d):
        start = (yy % 2) * NX
        return anc.at[0, yy // 2, pl.ds(start, NX) if k < 3 else pl.ds(start + (0 if d == 1 else 2), 2)]

    parts = (2, 1, 3)
    n_z = {part: number() for part in (1, 3)}
    n_xa = {d: number() for d in (1, 2, 3)}
    n_ya = {(k, d): number() for k in range(4) for d in (1, -1)}
    n_yb = {(part, d): number() for part in parts for d in range(1, NY)}
    n_xb = {(part, d): number() for part in parts for d in (1, 3)}
    n_xc = {(part, d): number() for part in parts for d in (1, 3)}

    def send_ya(*steps):
        for k in steps:
            for d in (1, -1):
                hop = (1, 2, 1, 2)[k]
                send(n_ya[k, d], line(wrap(y - d * (k + 1 - hop), NY), k, d), y_peer[d * hop % NY])

    def recv_ya(*steps):
        for k in steps:
            for d in (1, -1):
                recv(n_ya[k, d], line(wrap(y - d * (k + 1), NY), k, d), y_peer[d % NY])

    def send_xb(part, yy):
        block = cell(part, x, yy)
        for d in (1, 3):
            make(n_xb[part, d], block, block, x_peer[d]).start()

    def spread(part):
        for d in (1, 7, 2, 6, 3, 5, 4):
            send(n_yb[part, d], cell(part, x, y), y_peer[d])
        send_xb(part, y)

    def pass_on(part):
        for d in (1, 7, 2, 6, 3, 5, 4):
            yy = wrap(y - d, NY)
            recv(n_yb[part, d], cell(part, x, yy), y_peer[d])
            send_xb(part, yy)
        for d in (1, 3):
            sent.append(make(n_xb[part, d], column(part, x), column(part, x), x_peer[d]))

    def cross(part):
        for d in (1, 3):
            recv(n_xb[part, d], column(part, wrap(x - d, NX)), x_peer[d])
            send(n_xc[part, d], column(part, wrap(x - d, NX), 0 if d == 1 else 4, 4), x_peer[d])

    def recv_xc(part):
        for d in (1, 3):
            recv(n_xc[part, d], column(part, wrap(x + 2, NX), 0 if d == 1 else 4, 4), x_peer[d])

    for part, source in ((1, cell(0, x, y)), (3, cell(2, x, y))):
        send(n_z[part], source, partner, cell(part, x, y))
    for d in (1, 3, 2):
        send(n_xa[d], cell(0, x, y), x_peer[d])
    spread(2)
    temporal_queries(normed0, 0, 1)
    for d in (1, 3, 2):
        recv(n_xa[d], cell(0, wrap(x - d, NX), y), x_peer[d])
    send_ya(0, 1)
    for part in (1, 3):
        recv(n_z[part], cell(part, x, y), partner)
        spread(part)

    @pl.when(s != 0)
    def _():
        for d in range(1, NS):
            recv(n_frame[d], fr.at[wrap(s - d, NS)], at_space(wrap(s + d, NS)))
        normed = normalize(fr[...].reshape(NS * ROWS, C))
        kvs[...] = dot_t(normed, wsq[INNER:]).astype(BF)
        mixed = attend_space(head_queries(dot_t(normed, wsq[:WIDE])), kvs)
        sa_out[...] = mixed.reshape(NS, ROWS, WIDE)
        sa_in[s] = sa_out[s]

    for d in range(1, NS):
        there = wrap(s + d, NS)
        send_if(s != 0, n_back[d], sa_out.at[there], at_space(there), sa_in.at[s])

    pass_on(2)
    recv_ya(0, 1)
    send_ya(2, 3)
    pass_on(1)
    pass_on(3)
    cross(2)

    for d in range(1, NS):
        owner = wrap(s - d, NS)

        @pl.when(owner != 0)
        def _():
            recv(n_back[d], sa_in.at[owner], at_space(owner))

    rest = FRAMES - 1
    _, normed = temporal_rows(
        lat[1:].reshape(rest * ROWS, C), sa_in[1:].reshape(rest * ROWS, WIDE), 1, rest
    )
    n_next, n_prev = number(), number()
    send(n_next, tkv.at[pl.ds(FRAMES - 2, 2)], following, prev)
    send(n_prev, tkv.at[pl.ds(0, 2)], preceding, nxt)
    temporal_queries(normed, 1, rest)

    cross(1)
    cross(3)

    block = FRAMES * HALF
    row = lax.broadcasted_iota(jnp.int32, (HALF, 128), 0)
    lane = lax.broadcasted_iota(jnp.int32, (HALF, 128), 1)
    same = row == lane % HALF
    first = jnp.where(clip > 0, 0, 2 * HALF)
    last = jnp.where(clip < N_CLIP - 1, 4 * HALF, 2 * HALF)
    same_there = same & (lane >= first) & (lane < last)

    def attend(g, load, masks, start=False):
        queries = qm[g].reshape(HEADS * block, 128)
        tiles = [load(t) for t in range(5)]
        scores = jnp.concatenate(
            [
                dot_t(queries[:2 * block], tiles[0]),
                dot_t(queries[2 * block:4 * block], tiles[1]),
                dot_t(queries[4 * block:], tiles[2]),
            ],
            axis=0,
        )
        parts = []
        for i, mask in enumerate(masks):
            part = scores[:, 128 * i:128 * i + 128].reshape(-1, HALF, 128)
            parts.append(jnp.where(mask[None], part, NEG).reshape(HEADS * block, 128))
        high = parts[0]
        for part in parts[1:]:
            high = jnp.maximum(high, part)
        high = jnp.broadcast_to(jnp.max(high, axis=-1, keepdims=True), high.shape)
        if not start:
            high = jnp.maximum(high, top[g])
        parts = [jnp.exp(part - high) for part in parts]
        total = parts[0]
        for part in parts[1:]:
            total = total + part
        p = jnp.concatenate([part.astype(BF) for part in parts], axis=1)
        out = jnp.concatenate(
            [dot(p[:block], tiles[2]), dot(p[block:3 * block], tiles[3]), dot(p[3 * block:], tiles[4])], axis=0
        )
        if not start:
            shrink = jnp.exp(top[g] - high)
            total = total + tot[g] * shrink
            out = out + acc[g] * shrink
        top[g] = high
        tot[g] = total
        acc[g] = out

    def lanes(t):
        return pl.ds(128 * t, 128)

    def window(g, t):
        at = pl.ds(pl.multiple_of(HALF * g, HALF), HALF)
        own, before, after = [r[:, at, lanes(t)].reshape(-1, 128) for r in (tkv, prev, nxt)]
        return [own, before, after, before, after]

    def anchors(g, t, c):
        beside = (wrap(x + 1, NX), wrap(x - 1, NX))
        across = wrap(x + 2, NX)
        rows_a = [
            (y // 2, NX + x),
            (NX + beside[0], NX + beside[1]),
            (wrap(y // 2 + 1, NX), wrap(y // 2 - 1, NX)),
            (wrap(y // 2 + 2, NX), NX + across),
        ][c]
        rows_b = [NZ * xx for xx in (x, beside[0], beside[1], across)][c]
        rows = [jnp.where(g == 0, rows_a[i], rows_b + i) for i in range(2)]
        return [anc[g, r, :, :, lanes(t)].reshape(block, 128) for r in rows]

    def attend_anchors(g, chunks, start=False):
        def load(t):
            return jnp.concatenate([r for c in chunks for r in anchors(g, t, c)], axis=0)
        attend(g, load, [same, same] * len(chunks), start=start)

    def attend_window(g):
        def load(t):
            return jnp.concatenate(window(g, t), axis=0)
        attend(g, load, [same, same_there])

    def both(body, *args):
        def run(g, carry):
            body(g, *args)
            return carry
        lax.fori_loop(0, 2, run, 0)

    both(attend_anchors, (0,), True)
    recv_ya(2, 3)
    both(attend_anchors, (1, 2))
    recv(n_next, prev, preceding)
    recv(n_prev, nxt, following)
    both(attend_window)
    for part in parts:
        recv_xc(part)
    both(attend_anchors, (3,))

    for g in range(2):
        mixed = acc[g] / jnp.sum(tot[g], axis=-1, keepdims=True)
        mixed = side_by_side([mixed[h * block:(h + 1) * block] for h in range(HEADS)]).astype(BF)
        tatt[:, g] = mixed.reshape(FRAMES, HALF, WIDE)
    update = dot(tatt[...].reshape(FRAMES * ROWS, WIDE), wto[...])
    out = (spat[...].reshape(FRAMES * ROWS, C).astype(F32) + update).astype(BF)
    out_ref[...] = out.reshape(FRAMES, ROWS, C)
    for copy in sent:
        copy.wait_send()
    for cond, copy in conditional:
        @pl.when(cond)
        def _():
            copy.wait_send()
    assert count[0] <= COPIES


def step(latent, spatial_qkv, spatial_out, temporal_qkv, temporal_out):
    vmem = pltpu.VMEM
    tokens = FRAMES * HALF
    return pl.pallas_call(
        kernel,
        out_shape=jax.ShapeDtypeStruct(latent.shape, BF),
        in_specs=[pl.BlockSpec(memory_space=pl.ANY)] * 5,
        out_specs=pl.BlockSpec(memory_space=pltpu.VMEM),
        scratch_shapes=[
            vmem((FRAMES, ROWS, C), BF),
            vmem((3 * INNER, C), BF),
            vmem((WIDE, C), BF),
            vmem((3 * INNER, C), BF),
            vmem((WIDE, C), BF),
            vmem((NS, ROWS, C), BF),
            vmem((NS, ROWS, C), BF),
            vmem((NS * ROWS, 2 * INNER), BF),
            vmem((NS, ROWS, WIDE), BF),
            vmem((FRAMES, ROWS, WIDE), BF),
            vmem((2, 8, 8, HALF, 2 * INNER), BF),
            vmem((FRAMES, ROWS, 2 * INNER), BF),
            vmem((2, ROWS, 2 * INNER), BF),
            vmem((2, ROWS, 2 * INNER), BF),
            vmem((FRAMES, ROWS, C), BF),
            vmem((2, HEADS, FRAMES, HALF, 128), BF),
            vmem((2, HEADS * tokens, 128), F32),
            vmem((2, HEADS * tokens, 128), F32),
            vmem((2, HEADS * tokens, 128), F32),
            vmem((FRAMES, 2, HALF, WIDE), BF),
            pltpu.SemaphoreType.DMA((5,)),
            pltpu.SemaphoreType.DMA((COPIES,)),
            pltpu.SemaphoreType.DMA((COPIES,)),
        ],
        compiler_params=pltpu.CompilerParams(
            collective_id=0, has_side_effects=True, vmem_limit_bytes=60 * 1024 * 1024
        ),
        name="denoise",
    )(latent, spatial_qkv.T, spatial_out, temporal_qkv.T, temporal_out)


def solution(mesh):
    in_specs = (P("clip", "space", None), P(), P(), P(), P())
    out_specs = P("clip", "space", None)
    return jax.shard_map(step, mesh=mesh, in_specs=in_specs, out_specs=out_specs, check_vma=False)
```

```python
import jax
import jax.numpy as jnp
from jax import lax
from jax.experimental import pallas as pl
from jax.experimental.pallas import tpu as pltpu
from jax.sharding import PartitionSpec as P

MESH = pl.DeviceIdType.MESH
HEADS = 5
NZ, NY, NX = 2, 8, 4
N_CLIP = NZ * NY * NX
NS = 8
FRAMES = 8
ROWS = 32
HALF = 16
C = 640
INNER = 320
WIDE = 384
COPIES = 112
NEG = -1e30
BF = jnp.bfloat16
F32 = jnp.float32


def wrap(value, count):
    return lax.rem(value + 2 * count, count)


def normalize(values):
    wide = values.astype(F32)
    center = wide - jnp.mean(wide, axis=-1, keepdims=True)
    spread = jnp.mean(center * center, axis=-1, keepdims=True)
    return (center * lax.rsqrt(spread + 1e-05)).astype(BF)


def dot(a, b):
    return jnp.dot(a, b, preferred_element_type=F32)


def dot_t(a, b):
    return lax.dot_general(a, b, (((1,), (1,)), ((), ())), preferred_element_type=F32)


def low_lanes(rows):
    return lax.broadcasted_iota(jnp.int32, (rows, 128), 1) < 64


def head_queries(queries):
    low = low_lanes(queries.shape[0])
    tiles = []
    for h in range(HEADS):
        tile = queries[:, 128 * (h // 2):128 * (h // 2) + 128].astype(BF).astype(F32) * 0.125
        keep = low if h % 2 == 0 else jnp.logical_not(low)
        tiles.append(jnp.where(keep, tile, 0.0).astype(BF))
    return tiles


def side_by_side(heads):
    low = low_lanes(heads[0].shape[0])
    return jnp.concatenate(
        [
            jnp.where(low, 0.0, heads[0]),
            jnp.where(low, heads[1], heads[2]),
            jnp.where(low, heads[3], heads[4]),
        ],
        axis=1,
    )


def attend_space(queries, kv):
    heads = []
    for h in range(HEADS):
        kt, vt = 128 * (h // 2), 128 * (2 + (h + 1) // 2)
        scores = dot_t(queries[h], kv[:, kt:kt + 128])
        p = jnp.exp(scores - jnp.max(scores, axis=-1, keepdims=True))
        total = jnp.sum(p, axis=-1, keepdims=True)
        heads.append(dot(p.astype(BF), kv[:, vt:vt + 128]) / total)
    return side_by_side(heads).astype(BF)


def kernel(lat_h, wsq_h, wso_h, wtq_h, wto_h, out_ref,
           lat, wsq, wso, wtq, wto, f0, fr, kvs, sa_out, sa_in, anc, tkv, prev, nxt,
           spat, qm, acc, top, tot, tatt, lsem, ssem, rsem):
    clip = lax.axis_index("clip")
    s = lax.axis_index("space")
    zh, y, x = clip // (NY * NX), (clip // NX) % NY, clip % NX
    zl, core = s // 2, s % 2

    def at_clip(z_, y_, x_):
        return {"clip": (z_ * NY + y_) * NX + x_, "space": s}

    def at_space(s_):
        return {"clip": clip, "space": s_}

    partner = at_clip(1 - zh, y, x)
    x_peer = {d: at_clip(zh, y, wrap(x + d, NX)) for d in (1, 2, 3)}
    y_peer = {d: at_clip(zh, wrap(y + d, NY), x) for d in range(1, NY)}
    following = {"clip": wrap(clip + 1, N_CLIP), "space": s}
    preceding = {"clip": wrap(clip - 1, N_CLIP), "space": s}

    barrier = pltpu.get_barrier_semaphore()
    partners = [at_space(wrap(s + d, NS)) for d in range(1, NS)]
    partners += [partner] + [x_peer[d] for d in (1, 2, 3)] + [y_peer[d] for d in range(1, NY)] + [following, preceding]
    for device in partners:
        pl.semaphore_signal(barrier, inc=1, device_id=device, device_id_type=MESH)
    local = []

    def fetch(*pairs):
        for src, dst in pairs:
            copy = pltpu.make_async_copy(src, dst, lsem.at[len(local)])
            copy.start()
            local.append(copy)

    fetch((lat_h, lat))
    wso[0:64, :] = jnp.zeros((64, C), BF)
    wto[0:64, :] = jnp.zeros((64, C), BF)
    pl.semaphore_wait(barrier, len(partners))

    count = [0]
    sent = []

    def number():
        count[0] += 1
        return count[0] - 1

    def make(i, src, dst, device):
        return pltpu.make_async_remote_copy(
            src_ref=src, dst_ref=dst, send_sem=ssem.at[i], recv_sem=rsem.at[i], device_id=device, device_id_type=MESH
        )

    def send(i, ref, device, dst=None):
        copy = make(i, ref, ref if dst is None else dst, device)
        copy.start()
        sent.append(copy)

    def recv(i, ref, device):
        make(i, ref, ref, device).wait_recv()

    sibling = at_space(zl * 2 + 1 - core)
    same_core = {d: at_space(wrap(zl + d, 4) * 2 + core) for d in (1, 2, 3)}
    mine = lat_h.at[0]
    n_direct = {d: number() for d in (1, 2, 3)}
    n_relay = {d: number() for d in (1, 2, 3)}
    n_sib = number()
    for d in (2, 1, 3):
        send(n_direct[d], mine, same_core[d], f0.at[s])
    send(n_sib, mine, sibling, f0.at[s])
    fetch((wsq_h, wsq), (wso_h, wso.at[pl.ds(64, INNER)]), (wtq_h, wtq), (wto_h, wto.at[pl.ds(64, INNER)]))
    local[0].wait()
    f0[s] = lat[0]
    fr[s] = lat[s]
    for d in (1, 3, 2):
        slot = f0.at[wrap(zl - d, 4) * 2 + core]
        recv(n_direct[d], slot, same_core[d])
        send(n_relay[d], slot, sibling)

    n_frame = {d: number() for d in range(1, NS)}
    n_back = {d: number() for d in range(1, NS)}

    conditional = []

    def send_if(cond, i, src, device, dst):
        copy = make(i, src, dst, device)

        @pl.when(cond)
        def _():
            copy.start()

        conditional.append((cond, copy))

    recv(n_sib, f0.at[zl * 2 + 1 - core], sibling)
    for d in (1, 3, 2):
        recv(n_relay[d], f0.at[wrap(zl - d, 4) * 2 + 1 - core], sibling)

    def temporal_rows(latent, attn, first, frames):
        rows = frames * ROWS
        spatial = (latent.astype(F32) + dot(attn, wso[...])).astype(BF)
        spat[pl.ds(first, frames)] = spatial.reshape(frames, ROWS, C)
        normed = normalize(spatial)
        kv = dot_t(normed, wtq[INNER:]).astype(BF)
        tkv[pl.ds(first, frames)] = kv.reshape(frames, ROWS, 2 * INNER)
        return kv, normed

    def temporal_queries(normed, first, frames):
        for h, tile in enumerate(head_queries(dot_t(normed, wtq[:WIDE]))):
            tile = tile.reshape(frames, ROWS, 128)
            for g in range(2):
                qm[g, h, pl.ds(first, frames)] = tile[:, HALF * g:HALF * g + HALF]

    local[1].wait()
    queries0 = head_queries(dot_t(normalize(lat[0]), wsq[:WIDE]))
    kvs[...] = dot_t(normalize(f0[...].reshape(NS * ROWS, C)), wsq[INNER:]).astype(BF)
    mixed0 = attend_space(queries0, kvs)
    for copy in local[2:]:
        copy.wait()
    kv0, normed0 = temporal_rows(lat[0], mixed0, 0, 1)
    anc[0, y // 2, (y % 2) * NX + x] = kv0[:HALF]
    anc[1, NZ * x, y] = kv0[HALF:]

    def cell(part, xx, yy):
        if part == 0:
            return anc.at[0, yy // 2, (yy % 2) * NX + xx]
        if part == 1:
            return anc.at[0, NX + xx, yy]
        return anc.at[1, NZ * xx + part - 2, yy]

    def column(part, xx, *half):
        ref = anc.at[0, NX + xx] if part == 1 else anc.at[1, NZ * xx + part - 2]
        return ref.at[pl.ds(*half)] if half else ref

    def line(yy, k, d):
        start = (yy % 2) * NX
        return anc.at[0, yy // 2, pl.ds(start, NX) if k < 3 else pl.ds(start + (0 if d == 1 else 2), 2)]

    parts = (2, 1, 3)
    n_z = {part: number() for part in (1, 3)}
    n_xa = {d: number() for d in (1, 2, 3)}
    n_ya = {(k, d): number() for k in range(4) for d in (1, -1)}
    n_yb = {(part, d): number() for part in parts for d in range(1, NY)}
    n_xb = {(part, d): number() for part in parts for d in (1, 3)}
    n_xc = {(part, d): number() for part in parts for d in (1, 3)}

    def send_ya(*steps):
        for k in steps:
            for d in (1, -1):
                hop = (1, 2, 1, 2)[k]
                send(n_ya[k, d], line(wrap(y - d * (k + 1 - hop), NY), k, d), y_peer[d * hop % NY])

    def recv_ya(*steps):
        for k in steps:
            for d in (1, -1):
                recv(n_ya[k, d], line(wrap(y - d * (k + 1), NY), k, d), y_peer[d % NY])

    def send_xb(part, yy):
        block = cell(part, x, yy)
        for d in (1, 3):
            make(n_xb[part, d], block, block, x_peer[d]).start()

    def spread(part):
        for d in (1, 7, 2, 6, 3, 5, 4):
            send(n_yb[part, d], cell(part, x, y), y_peer[d])
        send_xb(part, y)

    def pass_on(part):
        for d in (1, 7, 2, 6, 3, 5, 4):
            yy = wrap(y - d, NY)
            recv(n_yb[part, d], cell(part, x, yy), y_peer[d])
            send_xb(part, yy)
        for d in (1, 3):
            sent.append(make(n_xb[part, d], column(part, x), column(part, x), x_peer[d]))

    def cross(part):
        for d in (1, 3):
            recv(n_xb[part, d], column(part, wrap(x - d, NX)), x_peer[d])
            send(n_xc[part, d], column(part, wrap(x - d, NX), 0 if d == 1 else 4, 4), x_peer[d])

    def recv_xc(part):
        for d in (1, 3):
            recv(n_xc[part, d], column(part, wrap(x + 2, NX), 0 if d == 1 else 4, 4), x_peer[d])

    for part, source in ((1, cell(0, x, y)), (3, cell(2, x, y))):
        send(n_z[part], source, partner, cell(part, x, y))
    for d in range(1, NS):
        owner = wrap(s + d, NS)
        send_if(owner != 0, n_frame[d], lat_h.at[owner], at_space(owner), fr.at[s])
    for d in (1, 3, 2):
        send(n_xa[d], cell(0, x, y), x_peer[d])
    spread(2)
    temporal_queries(normed0, 0, 1)
    for d in (1, 3, 2):
        recv(n_xa[d], cell(0, wrap(x - d, NX), y), x_peer[d])
    send_ya(0, 1)
    for part in (1, 3):
        recv(n_z[part], cell(part, x, y), partner)
        spread(part)

    @pl.when(s != 0)
    def _():
        for d in range(1, NS):
            recv(n_frame[d], fr.at[wrap(s - d, NS)], at_space(wrap(s + d, NS)))
        normed = normalize(fr[...].reshape(NS * ROWS, C))
        kvs[...] = dot_t(normed, wsq[INNER:]).astype(BF)
        mixed = attend_space(head_queries(dot_t(normed, wsq[:WIDE])), kvs)
        sa_out[...] = mixed.reshape(NS, ROWS, WIDE)
        sa_in[s] = sa_out[s]

    for d in range(1, NS):
        there = wrap(s + d, NS)
        send_if(s != 0, n_back[d], sa_out.at[there], at_space(there), sa_in.at[s])

    pass_on(2)
    recv_ya(0, 1)
    send_ya(2, 3)
    pass_on(1)
    pass_on(3)
    cross(2)

    for d in range(1, NS):
        owner = wrap(s - d, NS)

        @pl.when(owner != 0)
        def _():
            recv(n_back[d], sa_in.at[owner], at_space(owner))

    rest = FRAMES - 1
    _, normed = temporal_rows(
        lat[1:].reshape(rest * ROWS, C), sa_in[1:].reshape(rest * ROWS, WIDE), 1, rest
    )
    n_next, n_prev = number(), number()
    send(n_next, tkv.at[pl.ds(FRAMES - 2, 2)], following, prev)
    send(n_prev, tkv.at[pl.ds(0, 2)], preceding, nxt)

    cross(1)
    cross(3)
    temporal_queries(normed, 1, rest)

    block = FRAMES * HALF
    row = lax.broadcasted_iota(jnp.int32, (HALF, 128), 0)
    lane = lax.broadcasted_iota(jnp.int32, (HALF, 128), 1)
    same = row == lane % HALF
    first = jnp.where(clip > 0, 0, 2 * HALF)
    last = jnp.where(clip < N_CLIP - 1, 4 * HALF, 2 * HALF)
    same_there = same & (lane >= first) & (lane < last)

    def attend(g, load, masks, start=False):
        queries = qm[g].reshape(HEADS * block, 128)
        tiles = [load(t) for t in range(5)]
        scores = jnp.concatenate(
            [
                dot_t(queries[:2 * block], tiles[0]),
                dot_t(queries[2 * block:4 * block], tiles[1]),
                dot_t(queries[4 * block:], tiles[2]),
            ],
            axis=0,
        )
        parts = []
        for i, mask in enumerate(masks):
            part = scores[:, 128 * i:128 * i + 128].reshape(-1, HALF, 128)
            parts.append(jnp.where(mask[None], part, NEG).reshape(HEADS * block, 128))
        high = parts[0]
        for part in parts[1:]:
            high = jnp.maximum(high, part)
        high = jnp.broadcast_to(jnp.max(high, axis=-1, keepdims=True), high.shape)
        if not start:
            high = jnp.maximum(high, top[g])
        parts = [jnp.exp(part - high) for part in parts]
        total = parts[0]
        for part in parts[1:]:
            total = total + part
        p = jnp.concatenate([part.astype(BF) for part in parts], axis=1)
        out = jnp.concatenate(
            [dot(p[:block], tiles[2]), dot(p[block:3 * block], tiles[3]), dot(p[3 * block:], tiles[4])], axis=0
        )
        if not start:
            shrink = jnp.exp(top[g] - high)
            total = total + tot[g] * shrink
            out = out + acc[g] * shrink
        top[g] = high
        tot[g] = total
        acc[g] = out

    def lanes(t):
        return pl.ds(128 * t, 128)

    def window(g, t):
        at = pl.ds(pl.multiple_of(HALF * g, HALF), HALF)
        own, before, after = [r[:, at, lanes(t)].reshape(-1, 128) for r in (tkv, prev, nxt)]
        return [own, before, after, before, after]

    def anchors(g, t, c):
        beside = (wrap(x + 1, NX), wrap(x - 1, NX))
        across = wrap(x + 2, NX)
        rows_a = [
            (y // 2, NX + x),
            (NX + beside[0], NX + beside[1]),
            (wrap(y // 2 + 1, NX), wrap(y // 2 - 1, NX)),
            (wrap(y // 2 + 2, NX), NX + across),
        ][c]
        rows_b = [NZ * xx for xx in (x, beside[0], beside[1], across)][c]
        rows = [jnp.where(g == 0, rows_a[i], rows_b + i) for i in range(2)]
        return [anc[g, r, :, :, lanes(t)].reshape(block, 128) for r in rows]

    def attend_anchors(g, chunks, start=False):
        def load(t):
            return jnp.concatenate([r for c in chunks for r in anchors(g, t, c)], axis=0)
        attend(g, load, [same, same] * len(chunks), start=start)

    def attend_window(g):
        def load(t):
            return jnp.concatenate(window(g, t), axis=0)
        attend(g, load, [same, same_there])

    def both(body, *args):
        def run(g, carry):
            body(g, *args)
            return carry
        lax.fori_loop(0, 2, run, 0)

    both(attend_anchors, (0,), True)
    recv_ya(2, 3)
    both(attend_anchors, (1, 2))
    recv(n_next, prev, preceding)
    recv(n_prev, nxt, following)
    both(attend_window)
    for part in parts:
        recv_xc(part)
    both(attend_anchors, (3,))

    for g in range(2):
        mixed = acc[g] / jnp.sum(tot[g], axis=-1, keepdims=True)
        mixed = side_by_side([mixed[h * block:(h + 1) * block] for h in range(HEADS)]).astype(BF)
        tatt[:, g] = mixed.reshape(FRAMES, HALF, WIDE)
    update = dot(tatt[...].reshape(FRAMES * ROWS, WIDE), wto[...])
    out = (spat[...].reshape(FRAMES * ROWS, C).astype(F32) + update).astype(BF)
    out_ref[...] = out.reshape(FRAMES, ROWS, C)
    for copy in sent:
        copy.wait_send()
    for cond, copy in conditional:
        @pl.when(cond)
        def _():
            copy.wait_send()
    assert count[0] <= COPIES


def step(latent, spatial_qkv, spatial_out, temporal_qkv, temporal_out):
    vmem = pltpu.VMEM
    tokens = FRAMES * HALF
    return pl.pallas_call(
        kernel,
        out_shape=jax.ShapeDtypeStruct(latent.shape, BF),
        in_specs=[pl.BlockSpec(memory_space=pl.ANY)] * 5,
        out_specs=pl.BlockSpec(memory_space=pltpu.VMEM),
        scratch_shapes=[
            vmem((FRAMES, ROWS, C), BF),
            vmem((3 * INNER, C), BF),
            vmem((WIDE, C), BF),
            vmem((3 * INNER, C), BF),
            vmem((WIDE, C), BF),
            vmem((NS, ROWS, C), BF),
            vmem((NS, ROWS, C), BF),
            vmem((NS * ROWS, 2 * INNER), BF),
            vmem((NS, ROWS, WIDE), BF),
            vmem((FRAMES, ROWS, WIDE), BF),
            vmem((2, 8, 8, HALF, 2 * INNER), BF),
            vmem((FRAMES, ROWS, 2 * INNER), BF),
            vmem((2, ROWS, 2 * INNER), BF),
            vmem((2, ROWS, 2 * INNER), BF),
            vmem((FRAMES, ROWS, C), BF),
            vmem((2, HEADS, FRAMES, HALF, 128), BF),
            vmem((2, HEADS * tokens, 128), F32),
            vmem((2, HEADS * tokens, 128), F32),
            vmem((2, HEADS * tokens, 128), F32),
            vmem((FRAMES, 2, HALF, WIDE), BF),
            pltpu.SemaphoreType.DMA((5,)),
            pltpu.SemaphoreType.DMA((COPIES,)),
            pltpu.SemaphoreType.DMA((COPIES,)),
        ],
        compiler_params=pltpu.CompilerParams(
            collective_id=0, has_side_effects=True, vmem_limit_bytes=60 * 1024 * 1024
        ),
        name="denoise",
    )(latent, spatial_qkv.T, spatial_out, temporal_qkv.T, temporal_out)


def solution(mesh):
    in_specs = (P("clip", "space", None), P(), P(), P(), P())
    out_specs = P("clip", "space", None)
    return jax.shard_map(step, mesh=mesh, in_specs=in_specs, out_specs=out_specs, check_vma=False)
```
